768 devices in a mesh: seq: 64 (over x, y, core), head: 12 (over z).
Axes of the slice: x: 4, y: 8, z: 12, core: 2. Of those that a mesh axis runs over, the one named last changes fastest.
Arguments:
- queries: bfloat16 [12288, 6144], P('seq', 'head'), may hold values from -6 to 6, as said below
- keys: bfloat16 [12288, 768], P('seq'), may hold values from -6 to 6, as said below
- values: bfloat16 [12288, 768], P('seq'), may hold values from -6 to 6
- out_weight: bfloat16 [6144, 8192], P('head'), may hold values from -0.25 to 0.25
- doc_lengths: int32 [48], replicated, may hold values from 1 to 3072, 12288 in all
- pair_ids: int32 [48], replicated, may hold values from 0 to 23, never falling along the last dimension, each value on 1 to 3 neighbouring positions
- block_plan: int32 [2048], replicated, may hold values from 0 to 2047, as said below
Outputs:
- projected: bfloat16 [12288, 8192], P(('seq', 'head'))
The draws below stay inside these ranges and needn't reach their ends.
Inputs may be any that keep to these rules, and one draw needn't show every extreme that they name: Entries of queries lie in the range given. Entries of keys lie in the range given. `doc_lengths`: the lengths sum to 12288. `pair_ids`: never falling; every pair 0 to 23 holds one to three consecutive documents. `block_plan`: A permutation of the 2048 blocks of 6 tokens, numbered along the row. The 32 consecutive slots of one seq index hold blocks from 32 different seq indices, and the 32 blocks of one seq index go to 32 different seq indices.
All inputs are finite; a program needn't handle non-finite values.
Results may differ from the reference program's by a relative error of at most 0.015.
Values may be sent and summed in bfloat16 or wider, within the bound.
No kernel may reach another device: no remote copies, remote signals or barrier semaphores. Data moves between devices by JAX's collectives and lax.ppermute only.
A program may use at most 64 MiB of HBM per device.

```python
import math
import jax
import jax.numpy as jnp
import numpy as np
from jax import lax

D = 8192
D_HEAD = 128
QH_DEV = 4
TOK_DEV = 192
NDOC = 48
NPAIR = 24
KV_HEADS = 6
Q_HEADS = 48
NB = 32
BLK = 6
NBLK = 2048
SEQ_LEN = 12288
MAXDOC = 3072


def paired_rows(key):
    query_key, keys_key = jax.random.split(jax.random.fold_in(key, 31), 2)
    query_width = Q_HEADS * D_HEAD
    key_width = KV_HEADS * D_HEAD
    query_vals = jnp.clip(jax.random.normal(query_key, (SEQ_LEN, query_width), jnp.float32), -6.0, 6.0)
    key_vals = jnp.clip(jax.random.normal(keys_key, (SEQ_LEN, key_width), jnp.float32), -6.0, 6.0)
    return (query_vals, key_vals)


def draw_queries(key, part):
    return paired_rows(key)[0].astype(jnp.bfloat16)


def draw_keys(key, part):
    return paired_rows(key)[1].astype(jnp.bfloat16)


def draw_block_plan(key, part):
    device_count = SEQ_LEN // TOK_DEV
    first_key, second_key, third_key, fourth_key = jax.random.split(jax.random.fold_in(key, 53), 4)
    offsets = jax.random.permutation(first_key, device_count)[:NB].astype(jnp.int32)
    outer = jax.random.permutation(second_key, device_count).astype(jnp.int32)
    inner = jax.random.permutation(third_key, device_count).astype(jnp.int32)
    local_order = jax.random.permutation(fourth_key, NB).astype(jnp.int32)
    outer_inverse = jnp.argsort(outer).astype(jnp.int32)
    inner_inverse = jnp.argsort(inner).astype(jnp.int32)
    shifted = (outer_inverse[:, None] - offsets[None, :]) % device_count
    source = inner_inverse[shifted]
    plan = source * NB + local_order[None, :]
    return plan.reshape(-1).astype(jnp.int32)


def block_levels(stream_key, shape, cuts, low, high):
    def one(axis_at, shards_of):
        draws = jax.random.uniform(jax.random.fold_in(jax.random.fold_in(stream_key, 6), axis_at), (shards_of,), jnp.float32, low / len(cuts), high / len(cuts))
        return jnp.repeat(jnp.exp(draws), shape[axis_at] // shards_of).reshape((-1,) + (1,) * (len(shape) - axis_at - 1))

    level = one(*cuts[0])
    for cut in cuts[1:]:
        level = level * one(*cut)
    return level


def profile(amount, total, most, lean):
    weights = [(1 << 20) // math.isqrt(rank ** lean) + 1 for rank in range(2, amount + 1)]
    surplus, holding = total - most - (amount - 1), [1] * (amount - 1)
    while surplus > 0:
        movable = [i for i in range(amount - 1) if holding[i] < most]
        mass, budget = sum([weights[i] for i in movable]), surplus
        for i in movable:
            more = min(most - holding[i], max(1, budget * weights[i] // mass), surplus)
            holding[i] = holding[i] + more
            surplus = surplus - more
    return np.array([most] + holding)


def ragged(stream_key, count, total, bound, slope):
    if count == 2:
        one = jax.random.randint(stream_key, (), max(1, total - bound), min(bound, total - 1) + 1)
        return jnp.stack([one, total - one])
    lengths = jnp.asarray(profile(count, total, bound, slope), jnp.int32)
    pairs = (count - 1) // 2
    donor, receiver = lengths[1:1 + 2 * pairs:2], lengths[2:2 + 2 * pairs:2]
    room = jnp.minimum(donor - 1, bound - receiver)
    passed = jax.random.randint(jax.random.fold_in(stream_key, 1), (pairs,), 0, 1 << 20) % (room + 1)
    lengths = lengths.at[1:1 + 2 * pairs:2].set(donor - passed).at[2:2 + 2 * pairs:2].set(receiver + passed)
    return lengths[jax.random.permutation(jax.random.fold_in(stream_key, 2), count)]


def normal_values(own_key, extent, deviation, reach, cuts=(), kind=jnp.bfloat16):
    array = deviation * jax.random.normal(own_key, extent, jnp.float32)
    if cuts:
        array = array * block_levels(own_key, extent, cuts, -0.22, 0.18)
    return jnp.clip(array, -reach, reach).astype(kind)


def setup_inputs(seed: int = 0) -> dict:
    seeds = jax.random.split(jax.random.key(seed), 8)
    queries = draw_queries(jax.random.fold_in(seeds[7], 71), 0)
    keys = draw_keys(jax.random.fold_in(seeds[7], 71), 0)
    values = normal_values(seeds[2], (SEQ_LEN, KV_HEADS * D_HEAD), 1.0, 6.0, ((0, 64),))
    out_weight = normal_values(seeds[3], (Q_HEADS * D_HEAD, D), (QH_DEV * D_HEAD) ** -0.5, 0.25, ((0, 12),))
    doc_lengths = ragged(seeds[4], NDOC, SEQ_LEN, MAXDOC, 2).astype(jnp.int32)
    pair_ids = jnp.searchsorted(jnp.cumsum(ragged(seeds[5], NPAIR, NDOC, 3, 0)), jnp.arange(NDOC), side="right").astype(jnp.int32)
    block_plan = draw_block_plan(jax.random.fold_in(seeds[7], 71), 0)
    return {"queries": queries, "keys": keys, "values": values, "out_weight": out_weight, "doc_lengths": doc_lengths, "pair_ids": pair_ids, "block_plan": block_plan}


NEGATIVE = -1e+30

def token_docs(positions, doc_lengths):
    doc_ends = jnp.cumsum(doc_lengths)
    return lax.optimization_barrier(jnp.sum((doc_ends[None, :] <= positions[:, None]).astype(jnp.int32), axis=1))

def pair_firsts(docs, pair_ids):
    doc_range = jnp.arange(pair_ids.shape[0], dtype=jnp.int32)
    own_pair = lax.optimization_barrier(jnp.sum(jnp.where(docs[:, None] == doc_range[None, :], pair_ids[None, :], 0), axis=1))
    return lax.optimization_barrier(jnp.sum((pair_ids[None, :] < own_pair[:, None]).astype(jnp.int32), axis=1))

def reference(queries, keys, values, out_weight, doc_lengths, pair_ids, block_plan):
    positions = jnp.arange(SEQ_LEN, dtype=jnp.int32)
    docs_all = token_docs(positions, doc_lengths)
    firsts_all = pair_firsts(docs_all, pair_ids)
    scale = 1.0 / math.sqrt(D_HEAD)
    query_block = 4 * TOK_DEV
    block_total = SEQ_LEN // query_block
    group_total = Q_HEADS // QH_DEV

    def one_group(group_index):
        kv_index = group_index // 2
        key_rows = lax.dynamic_slice_in_dim(keys, (kv_index * D_HEAD).astype(jnp.int32), D_HEAD, 1).astype(jnp.float32)
        value_rows = lax.dynamic_slice_in_dim(values, (kv_index * D_HEAD).astype(jnp.int32), D_HEAD, 1).astype(jnp.float32)
        group_queries = lax.dynamic_slice_in_dim(queries, (group_index * QH_DEV * D_HEAD).astype(jnp.int32), QH_DEV * D_HEAD, 1)

        def one_block(block_index):
            start_row = (block_index * query_block).astype(jnp.int32)
            query_rows = lax.dynamic_slice_in_dim(group_queries, start_row, query_block, 0)
            query_rows = query_rows.astype(jnp.float32).reshape(query_block, QH_DEV, D_HEAD)
            row_pos = lax.dynamic_slice_in_dim(positions, start_row, query_block, 0)
            row_docs = lax.dynamic_slice_in_dim(docs_all, start_row, query_block, 0)
            row_firsts = lax.dynamic_slice_in_dim(firsts_all, start_row, query_block, 0)
            allowed = (positions[None, :] <= row_pos[:, None]) & ((docs_all[None, :] == row_docs[:, None]) | (docs_all[None, :] == row_firsts[:, None]))
            scores = jnp.einsum('qhd,kd->hqk', query_rows, key_rows) * scale
            row_max = lax.optimization_barrier(jnp.max(jnp.where(allowed[None], scores, NEGATIVE), axis=2))
            weights = jnp.where(allowed[None], jnp.exp(scores - row_max[:, :, None]), 0.0)
            denominator = lax.optimization_barrier(jnp.sum(weights, axis=2))
            rounded = lax.optimization_barrier(weights.astype(jnp.bfloat16)).astype(jnp.float32)
            combined = jnp.einsum('hqk,kd->hqd', rounded, value_rows) / denominator[:, :, None]
            return combined.transpose(1, 0, 2).reshape(query_block, QH_DEV * D_HEAD).astype(jnp.bfloat16)
        outputs = lax.map(one_block, jnp.arange(block_total, dtype=jnp.int32))
        return outputs.reshape(SEQ_LEN, QH_DEV * D_HEAD)
    grouped = lax.map(one_group, jnp.arange(group_total, dtype=jnp.int32))
    attended = grouped.transpose(1, 0, 2).reshape(SEQ_LEN, group_total * QH_DEV * D_HEAD)
    planned = attended.reshape(NBLK, BLK, group_total * QH_DEV * D_HEAD)[block_plan]
    planned = planned.reshape(SEQ_LEN, group_total, QH_DEV * D_HEAD)
    weight_groups = out_weight.reshape(group_total, QH_DEV * D_HEAD, D)

    def add_group(running_total, group_index):
        group_rows = lax.dynamic_index_in_dim(planned, group_index, 1, False)
        group_weight = lax.dynamic_index_in_dim(weight_groups, group_index, 0, False)
        partial_term = jnp.dot(group_rows, group_weight, preferred_element_type=jnp.float32).astype(jnp.bfloat16)
        return (running_total + lax.optimization_barrier(partial_term).astype(jnp.float32), None)
    summed, unused_out = lax.scan(add_group, jnp.zeros((SEQ_LEN, D), jnp.float32), jnp.arange(group_total, dtype=jnp.int32))
    return summed.astype(jnp.bfloat16)
```

```python
import functools
import math

import jax
import jax.numpy as jnp
from jax import lax
from jax.experimental import pallas as pl
from jax.experimental.pallas import tpu as pltpu
from jax.sharding import PartitionSpec as P

D_HEAD = 128
NEGATIVE = -1e30
LANES = 128
TILE = 64


def doc_tables(doc_lengths, pair_ids):
    count = doc_lengths.shape[0]
    order = jnp.arange(count, dtype=jnp.int32)
    starts = jnp.sum(jnp.where(order[None, :] < order[:, None], doc_lengths[None, :], 0), axis=1)
    firsts = jnp.sum((pair_ids[None, :] < pair_ids[:, None]).astype(jnp.int32), axis=1)
    return starts, starts + doc_lengths, firsts


def pick(onehot, table):
    return jnp.sum(jnp.where(onehot, table[None, :], 0), axis=1)


def attend_kernel(flags, q_ref, pos_ref, bias_ref, *refs, sides, tiles, heads, chunk, scale):
    keyed = [refs[3 * n:3 * n + 3] for n in range(sides)]
    out_ref, qa_ref, posr_ref, max_ref, sum_ref, acc_ref = refs[3 * sides:]
    step = pl.program_id(0)
    rows = TILE * heads

    @pl.when(step == 0)
    def _():
        for t in range(tiles):
            for h in range(heads):
                at = pl.ds(t * rows + h * TILE, TILE)
                tok = pl.ds(t * TILE, TILE)
                qa_ref[at, :D_HEAD] = q_ref[tok, h * D_HEAD:(h + 1) * D_HEAD]
                qa_ref[at, D_HEAD:] = bias_ref[tok, :]
                posr_ref[at, :] = jnp.broadcast_to(pos_ref[tok, :], (TILE, LANES))
        max_ref[...] = jnp.full_like(max_ref, NEGATIVE)
        sum_ref[...] = jnp.zeros_like(sum_ref)
        acc_ref[...] = jnp.zeros_like(acc_ref)

    per_step = keyed[0][0].shape[0] // chunk
    for side, (kv_ref, doc_ref, key_pos_ref) in enumerate(keyed):
        for c in range(per_step):
            span = slice(c * chunk, (c + 1) * chunk)
            for t in range(tiles):
                at = pl.ds(t * rows, rows)

                @pl.when(flags[t, side, step * per_step + c] > 0)
                def _(at=at, span=span, kv_ref=kv_ref, doc_ref=doc_ref, key_pos_ref=key_pos_ref):
                    k = jnp.concatenate([kv_ref[span, :D_HEAD], doc_ref[span, :]], axis=1)
                    s = lax.dot_general(
                        qa_ref[at, :], k, (((1,), (1,)), ((), ())),
                        preferred_element_type=jnp.float32,
                    )
                    row_pos = jnp.concatenate([posr_ref[at, :]] * (chunk // LANES), axis=1)
                    s = jnp.where(key_pos_ref[:, span] <= row_pos, s, NEGATIVE)
                    before = max_ref[at, :]
                    newest = jnp.maximum(before, jnp.max(s, axis=1, keepdims=True))
                    w = jnp.exp((s - jnp.concatenate([newest] * (chunk // LANES), axis=1)) * scale)
                    factor = jnp.exp((before - newest) * scale)
                    max_ref[at, :] = newest
                    sum_ref[at, :] = sum_ref[at, :] * factor + jnp.sum(w, axis=1, keepdims=True)
                    acc_ref[at, :] = acc_ref[at, :] * factor + jnp.dot(
                        w.astype(jnp.bfloat16), kv_ref[span, D_HEAD:],
                        preferred_element_type=jnp.float32,
                    )

    @pl.when(step == pl.num_programs(0) - 1)
    def _():
        for t in range(tiles):
            for h in range(heads):
                at = pl.ds(t * rows + h * TILE, TILE)
                out_ref[pl.ds(t * TILE, TILE), h * D_HEAD:(h + 1) * D_HEAD] = (
                    acc_ref[at, :] / sum_ref[at, :]
                ).astype(jnp.bfloat16)


def attend(q, pos, bias, flags, keyed, block, chunk):
    tokens, width = q.shape
    heads = width // D_HEAD
    keys = keyed[0][0].shape[0]
    rows = tokens * heads
    sides = len(keyed)
    whole = lambda a: pl.BlockSpec(a.shape, lambda i, f: (0, 0))
    part = lambda a: pl.BlockSpec((block, a.shape[1]), lambda i, f: (i, 0))
    line = pl.BlockSpec((1, block), lambda i, f: (0, i))
    key_specs, key_args = [], []
    for kv, doc, key_pos in keyed:
        key_specs += [part(kv), part(doc), line]
        key_args += [kv, doc, key_pos]
    return pl.pallas_call(
        functools.partial(
            attend_kernel, sides=sides, tiles=tokens // TILE, heads=heads, chunk=chunk,
            scale=1.0 / math.sqrt(D_HEAD),
        ),
        out_shape=jax.ShapeDtypeStruct((tokens, width), jnp.bfloat16),
        grid_spec=pltpu.PrefetchScalarGridSpec(
            num_scalar_prefetch=1,
            grid=(keys // block,),
            in_specs=[whole(q), whole(pos), whole(bias)] + key_specs,
            out_specs=whole(q),
            scratch_shapes=[
                pltpu.VMEM((rows, D_HEAD + LANES), jnp.bfloat16),
                pltpu.VMEM((rows, LANES), jnp.int32),
                pltpu.VMEM((rows, LANES), jnp.float32),
                pltpu.VMEM((rows, LANES), jnp.float32),
                pltpu.VMEM((rows, D_HEAD), jnp.float32),
            ],
        ),
        compiler_params=pltpu.CompilerParams(vmem_limit_bytes=40 * 2**20),
        cost_estimate=pl.CostEstimate(
            flops=2 * rows * sides * keys * 3 * D_HEAD,
            bytes_accessed=sides * keys * 3 * LANES * 2,
            transcendentals=rows * sides * keys,
        ),
        name="attend",
    )(flags, q, pos, bias, *key_args)


def on_device(queries, keys, values, out_weight, doc_lengths, pair_ids, block_plan):
    seq_count = lax.axis_size("seq")
    my_seq = lax.axis_index("seq")
    shared_head = lax.axis_index("head") // 2
    slots_here = seq_count // 2
    tok_rows, row_width = queries.shape
    block_rows = tok_rows // slots_here
    slot_total = block_plan.shape[0]
    heads = row_width // D_HEAD

    kv = jnp.concatenate(
        [
            lax.dynamic_slice_in_dim(keys, shared_head * D_HEAD, D_HEAD, 1),
            lax.dynamic_slice_in_dim(values, shared_head * D_HEAD, D_HEAD, 1),
        ],
        axis=1,
    )
    gathered = lax.all_gather(kv, "seq", axis=0, tiled=True)

    local_ids = my_seq * slots_here + jnp.arange(slots_here, dtype=jnp.int32)
    plan_rows = lax.dynamic_slice_in_dim(block_plan, my_seq * slots_here, slots_here, 0)
    pos = (
        plan_rows[:, None] * block_rows + jnp.arange(block_rows, dtype=jnp.int32)[None, :]
    ).reshape(-1)
    slot_range = jnp.arange(slot_total, dtype=jnp.int32)
    target_slot = jnp.sum(
        jnp.where(block_plan[None, :] == local_ids[:, None], slot_range[None, :], 0), axis=1
    )
    device_range = jnp.arange(seq_count, dtype=jnp.int32)
    send_table = ((target_slot // slots_here)[:, None] == device_range[None, :]).astype(
        jnp.bfloat16
    )
    take_table = ((plan_rows // slots_here)[:, None] == device_range[None, :]).astype(jnp.bfloat16)
    blocked = queries.reshape(slots_here, block_rows, row_width)
    arrived = lax.all_to_all(
        jnp.einsum("bn,bkw->nkw", send_table, blocked, preferred_element_type=jnp.float32).astype(
            jnp.bfloat16
        ),
        "seq",
        split_axis=0,
        concat_axis=0,
        tiled=True,
    )
    chosen = jnp.einsum("bn,nkw->bkw", take_table, arrived, preferred_element_type=jnp.float32)
    chosen = chosen.astype(jnp.bfloat16).reshape(tok_rows, row_width)

    count = doc_lengths.shape[0]
    starts, ends, firsts = doc_tables(doc_lengths, pair_ids)
    doc_range = jnp.arange(count, dtype=jnp.int32)
    in_doc = (starts[None, :] <= pos[:, None]) & (pos[:, None] < ends[None, :])
    own_first = pick(in_doc, firsts)
    in_first = doc_range[None, :] == own_first[:, None]
    bias = jnp.where(in_doc | in_first, 0.0, NEGATIVE).astype(jnp.bfloat16)
    bias = jnp.pad(bias, ((0, 0), (0, LANES - count)))

    row_total = gathered.shape[0]
    key_pos = jnp.arange(row_total, dtype=jnp.int32)
    pad_starts = jnp.pad(starts, (0, LANES - count), constant_values=2**30)
    pad_ends = jnp.pad(ends, (0, LANES - count), constant_values=2**30)
    key_doc = (
        (pad_starts[None, :] <= key_pos[:, None]) & (key_pos[:, None] < pad_ends[None, :])
    ).astype(jnp.bfloat16)

    block = 1536 if row_total % 1536 == 0 else row_total
    chunk = 768
    tiles = tok_rows // TILE
    low = chunk * jnp.arange(row_total // chunk, dtype=jnp.int32)[None, :]
    seen = (low <= pos[:, None]) & (
        (pick(in_doc, starts)[:, None] < low + chunk)
        | ((pick(in_first, starts)[:, None] < low + chunk) & (low < pick(in_first, ends)[:, None]))
    )
    flags = jnp.any(seen.reshape(tiles, 1, TILE, -1), axis=2).astype(jnp.int32)

    attended = attend(
        chosen, pos[:, None], bias, flags, [(gathered, key_doc, key_pos[None, :])], block, chunk
    )
    return lax.psum_scatter(
        jnp.dot(attended, out_weight, preferred_element_type=jnp.float32).astype(jnp.bfloat16),
        "head",
        scatter_dimension=0,
        tiled=True,
    )


def solution(mesh):
    return jax.shard_map(
        on_device,
        mesh=mesh,
        in_specs=(P("seq", "head"), P("seq", None), P("seq", None), P("head", None), P(), P(), P()),
        out_specs=P(("seq", "head"), None),
        check_vma=False,
    )
```

```python
import functools
import math

import jax
import jax.numpy as jnp
from jax import lax
from jax.experimental import pallas as pl
from jax.experimental.pallas import tpu as pltpu
from jax.sharding import PartitionSpec as P

D_HEAD = 128
NEGATIVE = -1e30
LOWEST = -3e38
LANES = 128
TILE = 64


def doc_tables(doc_lengths, pair_ids):
    count = doc_lengths.shape[0]
    order = jnp.arange(count, dtype=jnp.int32)
    starts = jnp.sum(jnp.where(order[None, :] < order[:, None], doc_lengths[None, :], 0), axis=1)
    firsts = jnp.sum((pair_ids[None, :] < pair_ids[:, None]).astype(jnp.int32), axis=1)
    return starts, starts + doc_lengths, firsts


def attend_kernel(*refs, tiles, heads, scale):
    (q_ref, peer_q_ref, pos_ref, bias_ref, own_ref, other_ref), refs = refs[:6], refs[6:]
    docs, places, refs = refs[:4], refs[4:8], refs[8:]
    mine_ref, theirs_ref, mine_lse_ref, theirs_lse_ref = refs[:4]
    qa_ref, posr_ref, max_ref, sum_ref, acc_ref = refs[4:]
    step = pl.program_id(0)
    rows = TILE * heads
    chunk = own_ref.shape[0]
    wide = chunk // LANES
    to_base_two = scale * math.log2(math.e)

    @pl.when(step == 0)
    def _():
        for group, source in enumerate((q_ref, peer_q_ref)):
            for t in range(tiles):
                for h in range(heads):
                    at = pl.ds((group * tiles + t) * rows + h * TILE, TILE)
                    tok = pl.ds(t * TILE, TILE)
                    qa_ref[at, :D_HEAD] = source[tok, h * D_HEAD:(h + 1) * D_HEAD]
                    qa_ref[at, D_HEAD:] = bias_ref[tok, :]
        for t in range(tiles):
            for h in range(heads):
                posr_ref[pl.ds(t * rows + h * TILE, TILE), :] = jnp.broadcast_to(
                    pos_ref[pl.ds(t * TILE, TILE), :], (TILE, LANES)
                )
        max_ref[...] = jnp.full_like(max_ref, LOWEST)
        sum_ref[...] = jnp.zeros_like(sum_ref)
        acc_ref[...] = jnp.zeros_like(acc_ref)

    for side, (doc_ref, place_ref) in enumerate(zip(docs, places)):
        kv_ref = (own_ref, other_ref)[side // 2]
        lane = side % 2 * 2 * D_HEAD
        k = jnp.concatenate([kv_ref[:, lane:lane + D_HEAD], doc_ref[...]], axis=1)
        v = kv_ref[:, lane + D_HEAD:lane + 2 * D_HEAD]
        for part in range(2 * tiles):
            at = pl.ds(part * rows, rows)
            s = lax.dot_general(
                qa_ref[at, :], k, (((1,), (1,)), ((), ())), preferred_element_type=jnp.float32
            )
            row_pos = posr_ref[pl.ds(part % tiles * rows, rows), :]
            s = jnp.where(place_ref[...] <= jnp.concatenate([row_pos] * wide, axis=1), s, NEGATIVE)
            before = max_ref[at, :]
            newest = jnp.maximum(before, jnp.max(s, axis=1, keepdims=True))
            w = jnp.exp2((s - jnp.concatenate([newest] * wide, axis=1)) * to_base_two)
            factor = jnp.exp2((before - newest) * to_base_two)
            max_ref[at, :] = newest
            sum_ref[at, :] = sum_ref[at, :] * factor + jnp.sum(w, axis=1, keepdims=True)
            acc_ref[at, :] = acc_ref[at, :] * factor + jnp.dot(
                w.astype(jnp.bfloat16), v, preferred_element_type=jnp.float32
            )

    @pl.when(step == pl.num_programs(0) - 1)
    def _():
        column = lax.broadcasted_iota(jnp.int32, (TILE, LANES), 1)
        ends = ((mine_ref, mine_lse_ref), (theirs_ref, theirs_lse_ref))
        for group, (out_ref, lse_ref) in enumerate(ends):
            for t in range(tiles):
                tok = pl.ds(t * TILE, TILE)
                lse = jnp.zeros((TILE, LANES), jnp.float32)
                for h in range(heads):
                    at = pl.ds((group * tiles + t) * rows + h * TILE, TILE)
                    total = sum_ref[at, :]
                    out_ref[tok, h * D_HEAD:(h + 1) * D_HEAD] = (acc_ref[at, :] / total).astype(
                        out_ref.dtype
                    )
                    lse = jnp.where(column == h, max_ref[at, :] * scale + jnp.log(total), lse)
                lse_ref[tok, :] = lse


def attend(q, peer_q, pos, bias, own, other, docs, places, chunk):
    tokens, width = q.shape
    heads = width // D_HEAD
    keys = own.shape[0]
    rows = 2 * tokens * heads
    whole = lambda a: pl.BlockSpec(a.shape, lambda i: (0, 0))
    part = lambda a: pl.BlockSpec((chunk, a.shape[1]), lambda i: (i, 0))
    line = pl.BlockSpec((1, chunk), lambda i: (0, i))
    outs = [
        jax.ShapeDtypeStruct((tokens, width), jnp.float32),
        jax.ShapeDtypeStruct((tokens, width), jnp.bfloat16),
        jax.ShapeDtypeStruct((tokens, LANES), jnp.float32),
        jax.ShapeDtypeStruct((tokens, LANES), jnp.float32),
    ]
    return pl.pallas_call(
        functools.partial(
            attend_kernel, tiles=tokens // TILE, heads=heads, scale=1.0 / math.sqrt(D_HEAD)
        ),
        out_shape=outs,
        grid=(keys // chunk,),
        in_specs=[whole(q), whole(peer_q), whole(pos), whole(bias), part(own), part(other)]
        + [part(d) for d in docs]
        + [line] * 4,
        out_specs=[whole(o) for o in outs],
        scratch_shapes=[
            pltpu.VMEM((rows, D_HEAD + LANES), jnp.bfloat16),
            pltpu.VMEM((rows // 2, LANES), jnp.int32),
            pltpu.VMEM((rows, LANES), jnp.float32),
            pltpu.VMEM((rows, LANES), jnp.float32),
            pltpu.VMEM((rows, D_HEAD), jnp.float32),
        ],
        compiler_params=pltpu.CompilerParams(vmem_limit_bytes=40 * 2**20),
        cost_estimate=pl.CostEstimate(
            flops=2 * rows * 4 * keys * 3 * D_HEAD,
            bytes_accessed=4 * keys * 3 * LANES * 2,
            transcendentals=rows * 4 * keys,
        ),
        name="attend",
    )(q, peer_q, pos, bias, own, other, *docs, *places)


def merge_project_kernel(mine_ref, theirs_ref, mine_lse_ref, theirs_lse_ref, w_ref, out_ref, joined_ref):
    @pl.when(pl.program_id(0) == 0)
    def _():
        a, b = mine_lse_ref[...], theirs_lse_ref[...]
        top = jnp.maximum(a, b)
        a, b = jnp.exp(a - top), jnp.exp(b - top)
        share = a / (a + b)
        rest = b / (a + b)
        for h in range(mine_ref.shape[1] // D_HEAD):
            span = slice(h * D_HEAD, (h + 1) * D_HEAD)
            joined_ref[:, span] = (
                mine_ref[:, span] * share[:, h:h + 1]
                + theirs_ref[:, span].astype(jnp.float32) * rest[:, h:h + 1]
            ).astype(jnp.bfloat16)

    out_ref[...] = jnp.dot(
        joined_ref[...], w_ref[...], preferred_element_type=jnp.float32
    ).astype(jnp.bfloat16)


def merge_project(mine, theirs, mine_lse, theirs_lse, weight):
    tokens, depth = mine.shape
    width = weight.shape[1]
    columns = min(width, 1024)
    whole = lambda a: pl.BlockSpec(a.shape, lambda i: (0, 0))
    return pl.pallas_call(
        merge_project_kernel,
        out_shape=jax.ShapeDtypeStruct((tokens, width), jnp.bfloat16),
        grid=(width // columns,),
        in_specs=[
            whole(mine), whole(theirs), whole(mine_lse), whole(theirs_lse),
            pl.BlockSpec((depth, columns), lambda i: (0, i)),
        ],
        out_specs=pl.BlockSpec((tokens, columns), lambda i: (0, i)),
        scratch_shapes=[pltpu.VMEM((tokens, depth), jnp.bfloat16)],
        compiler_params=pltpu.CompilerParams(vmem_limit_bytes=32 * 2**20),
        cost_estimate=pl.CostEstimate(
            flops=2 * tokens * depth * width,
            bytes_accessed=2 * (depth + tokens) * width,
            transcendentals=0,
        ),
        name="merge_project",
    )(mine, theirs, mine_lse, theirs_lse, weight)


def on_device(queries, keys, values, out_weight, doc_lengths, pair_ids, block_plan):
    seq_count = lax.axis_size("seq")
    head_count = lax.axis_size("head")
    my_seq = lax.axis_index("seq")
    my_head = lax.axis_index("head")
    my_core = lax.rem(my_seq, 2)
    my_half = lax.rem(my_head, 2)
    slots_here = seq_count // 2
    tok_rows, row_width = queries.shape
    block_rows = tok_rows // slots_here
    slot_total = block_plan.shape[0]
    quarter = tok_rows // 4
    eighth = quarter // 2

    column = my_head // 2 * D_HEAD
    first_row = my_half * 2 * quarter
    kv = jnp.concatenate(
        [
            lax.dynamic_slice(keys, (first_row, column), (2 * quarter, D_HEAD)),
            lax.dynamic_slice(values, (first_row, column), (2 * quarter, D_HEAD)),
        ],
        axis=1,
    )
    by_core = jnp.stack(
        [
            jnp.concatenate([kv[c * quarter:c * quarter + eighth], kv[c * quarter + eighth:(c + 1) * quarter]], axis=1)
            for c in range(2)
        ]
    )
    kv_sent = jnp.broadcast_to(by_core[None], (seq_count // 2, 2, eighth, 4 * D_HEAD)).reshape(
        seq_count, eighth, 4 * D_HEAD
    )

    local_ids = my_seq * slots_here + jnp.arange(slots_here, dtype=jnp.int32)
    plan_rows = lax.dynamic_slice_in_dim(block_plan, my_seq * slots_here, slots_here, 0)
    pos = (
        plan_rows[:, None] * block_rows + jnp.arange(block_rows, dtype=jnp.int32)[None, :]
    ).reshape(-1)
    slot_range = jnp.arange(slot_total, dtype=jnp.int32)
    target_slot = jnp.sum(
        jnp.where(block_plan[None, :] == local_ids[:, None], slot_range[None, :], 0), axis=1
    )
    device_range = jnp.arange(seq_count, dtype=jnp.int32)
    send_table = ((target_slot // slots_here)[:, None] == device_range[None, :]).astype(
        jnp.bfloat16
    )
    take_table = ((plan_rows // slots_here)[:, None] == device_range[None, :]).astype(jnp.bfloat16)
    blocked = queries.reshape(slots_here, block_rows, row_width)
    q_sent = jnp.einsum("bn,bkw->nkw", send_table, blocked, preferred_element_type=jnp.float32)
    q_room = -(-block_rows // 8) * 8
    q_sent = jnp.pad(q_sent.astype(jnp.bfloat16), ((0, 0), (0, q_room - block_rows), (0, 0)))

    arrived = lax.all_to_all(
        jnp.concatenate([kv_sent, q_sent], axis=1), "seq", split_axis=0, concat_axis=0, tiled=True
    )
    own = arrived[:, :eighth].reshape(seq_count * eighth, 4 * D_HEAD)
    other = lax.ppermute(own, "seq", [(s, s ^ 1) for s in range(seq_count)])
    q_arrived = arrived[:, eighth:eighth + block_rows]
    chosen = jnp.einsum("bn,nkw->bkw", take_table, q_arrived, preferred_element_type=jnp.float32)
    chosen = chosen.astype(jnp.bfloat16).reshape(tok_rows, row_width)
    across = [(h, h ^ 1) for h in range(head_count)]
    peer_chosen = lax.ppermute(chosen, "head", across)

    count = doc_lengths.shape[0]
    starts, ends, firsts = doc_tables(doc_lengths, pair_ids)
    doc_range = jnp.arange(count, dtype=jnp.int32)
    in_doc = (starts[None, :] <= pos[:, None]) & (pos[:, None] < ends[None, :])
    own_first = jnp.sum(jnp.where(in_doc, firsts[None, :], 0), axis=1)
    in_first = doc_range[None, :] == own_first[:, None]
    bias = jnp.where(in_doc | in_first, 0.0, NEGATIVE).astype(jnp.bfloat16)
    bias = jnp.pad(bias, ((0, 0), (0, LANES - count)))

    per_side = seq_count * eighth
    entry = jnp.arange(per_side, dtype=jnp.int32)
    pad_starts = jnp.pad(starts, (0, LANES - count), constant_values=2**30)
    pad_ends = jnp.pad(ends, (0, LANES - count), constant_values=2**30)
    docs, places = [], []
    for core in (my_core, 1 - my_core):
        for part in range(2):
            offset = (2 * my_half + core) * quarter + part * eighth
            place = entry // eighth * tok_rows + offset + entry % eighth
            member = (pad_starts[None, :] <= place[:, None]) & (place[:, None] < pad_ends[None, :])
            docs.append(member.astype(jnp.bfloat16))
            places.append(place[None, :])

    chunk = 768 if per_side % 768 == 0 else per_side
    mine, theirs, mine_lse, theirs_lse = attend(
        chosen, peer_chosen, pos[:, None], bias, own, other, docs, places, chunk
    )
    term = merge_project(
        mine,
        lax.ppermute(theirs, "head", across),
        mine_lse,
        lax.ppermute(theirs_lse, "head", across),
        out_weight,
    )
    return lax.psum_scatter(term, "head", scatter_dimension=0, tiled=True)


def solution(mesh):
    return jax.shard_map(
        on_device,
        mesh=mesh,
        in_specs=(P("seq", "head"), P("seq", None), P("seq", None), P("head", None), P(), P(), P()),
        out_specs=P(("seq", "head"), None),
        check_vma=False,
    )
```
